256 devices in a mesh: row: 8 (over z_lo, core), col: 32 (over x, y, z_hi).
Axes of the slice: x: 4, y: 4, z: 8 (z_hi: 2, z_lo: 4; z = z_hi * 4 + z_lo), core: 2. Of those that a mesh axis runs over, the one named last changes fastest.
Arguments:
- tokens: bfloat16 [1024, 8192], P('col', 'row'), may hold values from -6 to 6
- gate_weight: bfloat16 [8192, 14336], P('row', 'col'), may hold values from -0.0625 to 0.0625
- up_weight: bfloat16 [8192, 14336], P('row', 'col'), may hold values from -0.0625 to 0.0625
- down_weight: bfloat16 [14336, 8192], P('col', 'row'), may hold values from -0.046875 to 0.046875
- grad_out: bfloat16 [1024, 8192], P('col', 'row'), may hold values from -3 to 3
Outputs:
- output: bfloat16 [1024, 8192], P('col', 'row')
- token_grad: bfloat16 [1024, 8192], P('col', 'row')
- gate_grad: bfloat16 [8192, 14336], P('row', 'col')
- up_grad: bfloat16 [8192, 14336], P('row', 'col')
- down_grad: bfloat16 [14336, 8192], P('col', 'row')
The draws below stay inside these ranges and needn't reach their ends.
All inputs are finite; a program needn't handle non-finite values.
Results may differ from the reference program's by a relative error of at most 0.0049.
Values may be sent and summed in bfloat16 or wider, within the bound.
No kernel may reach another device: no remote copies, remote signals or barrier semaphores. Data moves between devices by JAX's collectives and lax.ppermute only.
A program may use at most 128 MiB of HBM per device.

```python
import jax
import jax.numpy as jnp

D = 8192
FF = 14336
TOKENS = 1024


def level_of(own_key, shape, cuts, least, top_value):
    def one(position, shards_of):
        heights = jax.random.uniform(jax.random.fold_in(jax.random.fold_in(own_key, 6), position), (shards_of,), jnp.float32, least / len(cuts), top_value / len(cuts))
        return jnp.repeat(jnp.exp(heights), shape[position] // shards_of).reshape((-1,) + (1,) * (len(shape) - position - 1))

    level = one(*cuts[0])
    for cut in cuts[1:]:
        level = level * one(*cut)
    return level


def scatter_about(key, extent, spread, most, split=(), held_as=jnp.bfloat16):
    result = jax.random.normal(key, extent, jnp.float32) * spread
    if len(split) > 0:
        result = level_of(key, extent, split, -0.22, 0.18) * result
    return jnp.clip(result, min=-most, max=most).astype(held_as)


def setup_inputs(seed: int = 0) -> dict:
    streams_of = jax.random.split(jax.random.key(seed), 6)
    return {
        "tokens": scatter_about(streams_of[0], (TOKENS, D), 1.0, 6.0, ((0, 32), (1, 8))),
        "gate_weight": scatter_about(streams_of[1], (D, FF), D ** -0.5, 0.0625, ((0, 8), (1, 32))),
        "up_weight": scatter_about(streams_of[2], (D, FF), D ** -0.5, 0.0625, ((0, 8), (1, 32))),
        "down_weight": scatter_about(streams_of[3], (FF, D), FF ** -0.5, 0.046875, ((0, 32), (1, 8))),
        "grad_out": scatter_about(streams_of[4], (TOKENS, D), 0.5, 3.0, ((0, 32), (1, 8))),
    }


def reference(tokens, gate_weight, up_weight, down_weight, grad_out):
    gate_pre = jnp.dot(tokens, gate_weight, preferred_element_type=jnp.float32)
    up_pre = jnp.dot(tokens, up_weight, preferred_element_type=jnp.float32)
    hidden = (jax.nn.silu(gate_pre) * up_pre).astype(jnp.bfloat16)
    output = jnp.dot(hidden, down_weight, preferred_element_type=jnp.float32).astype(jnp.bfloat16)
    down_grad = jnp.dot(hidden.T, grad_out, preferred_element_type=jnp.float32).astype(jnp.bfloat16)
    hidden_grad = jnp.dot(grad_out, down_weight.T, preferred_element_type=jnp.float32)
    sigmoid_gate = jax.nn.sigmoid(gate_pre)
    gate_delta = (hidden_grad * up_pre * sigmoid_gate * (1.0 + gate_pre * (1.0 - sigmoid_gate))).astype(jnp.bfloat16)
    up_delta = (hidden_grad * gate_pre * sigmoid_gate).astype(jnp.bfloat16)
    gate_grad = jnp.dot(tokens.T, gate_delta, preferred_element_type=jnp.float32).astype(jnp.bfloat16)
    up_grad = jnp.dot(tokens.T, up_delta, preferred_element_type=jnp.float32).astype(jnp.bfloat16)
    token_grad = jnp.dot(gate_delta, gate_weight.T, preferred_element_type=jnp.float32)
    token_grad = token_grad + jnp.dot(up_delta, up_weight.T, preferred_element_type=jnp.float32)
    return output, token_grad.astype(jnp.bfloat16), gate_grad, up_grad, down_grad
```

```python
import jax
import jax.numpy as jnp
from jax import lax
from jax.sharding import PartitionSpec as P

F32 = jnp.float32
BF16 = jnp.bfloat16

XY_GROUPS = [[xy * 2 + hi for xy in range(16)] for hi in range(2)]
HI_SWAP = [(i, i ^ 1) for i in range(32)]
CORE_SWAP = [(i, i ^ 1) for i in range(8)]


def dot(left, right, dims):
    return lax.dot_general(left, right, ((dims[:1], dims[1:]), ((), ())), preferred_element_type=F32)


def z_swap(value, hop):
    return lax.ppermute(value, "row", [(i, i ^ (2 * hop)) for i in range(8)])


def gather_xy(block):
    copies = jnp.broadcast_to(block[None], (16,) + block.shape)
    every = lax.all_to_all(copies, "col", 0, 0, axis_index_groups=XY_GROUPS, tiled=True)
    return every.reshape(16 * block.shape[0], block.shape[1])


def reduce_xy(partial):
    blocks = partial.astype(BF16).reshape(16, partial.shape[0] // 16, partial.shape[1])
    every = lax.all_to_all(blocks, "col", 0, 0, axis_index_groups=XY_GROUPS, tiled=True)
    return jnp.sum(every.astype(F32), axis=0)


def reduce_row(keep, send, z_at):
    both = keep + lax.ppermute(send, "row", CORE_SWAP)
    width = both.shape[1] // 4

    def block(at):
        return lax.dynamic_slice_in_dim(both, at * width, width, axis=1)

    total = block(z_at)
    for hop in (2, 3, 1):
        total = total + z_swap(block(z_at ^ hop).astype(BF16), hop).astype(F32)
    return total


def gather_row(share, z_at):
    slots = [share] + [z_swap(share, hop) for hop in (1, 2, 3)]
    blocks = []
    for at in range(4):
        block = slots[at]
        for z in (1, 2, 3):
            block = jnp.where(z_at == z, slots[at ^ z], block)
        blocks.append(block)
    mine = jnp.concatenate(blocks, axis=1)
    return mine, lax.ppermute(mine, "row", CORE_SWAP)


def on_device(tokens, gate_weight, up_weight, down_weight, grad_out):
    row = lax.axis_index("row")
    z_at, core = row // 2, row % 2
    half = gate_weight.shape[1] // 2

    gate_t, up_t = gate_weight.T, up_weight.T
    joined = jnp.stack(
        [jnp.concatenate([gate_t[i * half : (i + 1) * half], up_t[i * half : (i + 1) * half]], axis=0) for i in range(2)]
    )
    in_mine = lax.dynamic_index_in_dim(joined, core, 0, keepdims=False)
    in_other = lax.dynamic_index_in_dim(joined, 1 - core, 0, keepdims=False)
    halves = down_weight.reshape(2, half, down_weight.shape[1])
    down_mine = lax.dynamic_index_in_dim(halves, core, 0, keepdims=False)
    down_other = lax.dynamic_index_in_dim(halves, 1 - core, 0, keepdims=False)

    blocks = [
        (tokens, grad_out),
        (lax.ppermute(tokens, "col", HI_SWAP), lax.ppermute(grad_out, "col", HI_SWAP)),
    ]
    sums = []
    kept = []
    for token_block, grad_block in blocks:
        tok, grad = gather_xy(token_block), gather_xy(grad_block)
        pre = reduce_row(dot(in_mine, tok, (1, 1)), dot(in_other, tok, (1, 1)), z_at)
        hidden_grad = reduce_row(dot(down_mine, grad, (1, 1)), dot(down_other, grad, (1, 1)), z_at)
        gate_pre, up_pre = pre[:half], pre[half:]
        sigmoid_gate = jax.nn.sigmoid(gate_pre)
        hidden = (jax.nn.silu(gate_pre) * up_pre).astype(BF16)
        gate_delta = (hidden_grad * up_pre * sigmoid_gate * (1.0 + gate_pre * (1.0 - sigmoid_gate))).astype(BF16)
        up_delta = (hidden_grad * gate_pre * sigmoid_gate).astype(BF16)
        hid_mine, hid_other = gather_row(hidden, z_at)
        output = reduce_xy(dot(hid_mine, down_mine, (0, 0)) + dot(hid_other, down_other, (0, 0)))
        delta_mine, delta_other = gather_row(jnp.concatenate([gate_delta, up_delta], axis=0), z_at)
        token_grad = reduce_xy(dot(delta_mine, in_mine, (0, 0)) + dot(delta_other, in_other, (0, 0)))
        sums.append((output, token_grad))

        def in_order(mine, other):
            return jnp.concatenate([jnp.where(core == 0, mine, other), jnp.where(core == 0, other, mine)], axis=0)

        kept.append(
            (
                tok,
                grad,
                in_order(hid_mine, hid_other),
                in_order(delta_mine[:half], delta_other[:half]),
                in_order(delta_mine[half:], delta_other[half:]),
            )
        )
    output, token_grad = (
        (own + lax.ppermute(other.astype(BF16), "col", HI_SWAP).astype(F32)).astype(BF16)
        for own, other in zip(*sums)
    )
    down_grad = sum(dot(hid, grad, (1, 0)) for _, grad, hid, _, _ in kept).astype(BF16)
    gate_grad = sum(dot(tok, delta, (0, 1)) for tok, _, _, delta, _ in kept).astype(BF16)
    up_grad = sum(dot(tok, delta, (0, 1)) for tok, _, _, _, delta in kept).astype(BF16)
    return output, token_grad, gate_grad, up_grad, down_grad


def solution(mesh):
    by_token, by_hidden = P("col", "row"), P("row", "col")
    return jax.shard_map(
        on_device,
        mesh=mesh,
        in_specs=(by_token, by_hidden, by_hidden, by_token, by_token),
        out_specs=(by_token, by_token, by_hidden, by_hidden, by_token),
        check_vma=False,
    )
```

```python
import jax
import jax.numpy as jnp
from jax import lax
from jax.experimental import pallas as pl
from jax.experimental.pallas import tpu as pltpu
from jax.sharding import PartitionSpec as P

F32 = jnp.float32
BF16 = jnp.bfloat16

HI_SWAP = [(i, i ^ 1) for i in range(32)]
CORE_SWAP = [(i, i ^ 1) for i in range(8)]


def dot(left, right, dims):
    return lax.dot_general(left, right, ((dims[:1], dims[1:]), ((), ())), preferred_element_type=F32)


def together(*values):
    return lax.optimization_barrier(values)


def core_swap(value):
    return lax.ppermute(value, "row", CORE_SWAP)


def hi_swap(value):
    return lax.ppermute(value, "col", HI_SWAP)


def z_swap(value, hop):
    return lax.ppermute(value, "row", [(i, i ^ (2 * hop)) for i in range(8)])


def xy_move(value, hop, core_on_x):
    pairs = []
    for row in range(8):
        for x in range(4):
            for y in range(4):
                to_x, to_y = ((x + hop) % 4, y) if row % 2 == core_on_x else (x, (y + hop) % 4)
                for hi in range(2):
                    pairs.append((row * 32 + (x * 4 + y) * 2 + hi, row * 32 + (to_x * 4 + to_y) * 2 + hi))
    return lax.ppermute(value, ("row", "col"), pairs)


def spread(value, core_on_x):
    moved = {hop: xy_move(value, hop, core_on_x) for hop in (2, 1, 3)}
    return [value] + [moved[hop] for hop in (1, 2, 3)]


def place_kernel(at, *refs):
    *lines, out = refs
    x, y, core = at[0], at[1], at[2]
    for e in range(4):
        for d in range(4):
            from_x = lax.rem(x + 4 - jnp.where(core == 1, e, d), 4)
            from_y = lax.rem(y + 4 - jnp.where(core == 1, d, e), 4)
            out[from_x * 4 + from_y] = lines[e][d]


def join_xy(lines, at):
    _, t, d = lines[0].shape
    out = pl.pallas_call(
        place_kernel,
        out_shape=jax.ShapeDtypeStruct((16, t, d), lines[0].dtype),
        in_specs=[pl.BlockSpec(memory_space=pltpu.SMEM)] + [pl.BlockSpec(memory_space=pltpu.VMEM)] * 4,
        out_specs=pl.BlockSpec(memory_space=pltpu.VMEM),
        compiler_params=pltpu.CompilerParams(vmem_limit_bytes=16 * 1024 * 1024),
        cost_estimate=pl.CostEstimate(flops=0, bytes_accessed=64 * t * d, transcendentals=0),
    )(at, *lines)
    return out.reshape(16 * t, d)


def cut(partial, at):
    blocks = partial.reshape(4, 4, -1, partial.shape[1])

    def piece(hop):
        along_x = lax.dynamic_index_in_dim(blocks, (at[0] + 4 - hop) % 4, 0, keepdims=False)
        along_y = lax.dynamic_index_in_dim(blocks, (at[1] + 4 - hop) % 4, 1, keepdims=False)
        return jnp.where(at[2] == 1, along_x, along_y)

    return [piece(0)] + [piece(hop).astype(BF16) for hop in (1, 2, 3)]


def cut_again(sums, at):
    place = jnp.where(at[2] == 1, at[1], at[0])
    pieces = [lax.dynamic_index_in_dim(sums, (place + 4 - hop) % 4, 0, keepdims=False) for hop in range(4)]
    return [pieces[0]] + [piece.astype(BF16) for piece in pieces[1:]]


def collect(pieces, core_on_x):
    moved = {hop: xy_move(pieces[hop].astype(BF16), -hop, core_on_x) for hop in (2, 1, 3)}
    return [pieces[0]] + [moved[hop] for hop in (1, 2, 3)]


def total(parts):
    return parts[0] + parts[1].astype(F32) + parts[2].astype(F32) + parts[3].astype(F32)


def scatter_z(both, z_at):
    width = both.shape[1] // 4

    def block(at):
        return lax.dynamic_slice_in_dim(both, at * width, width, axis=1)

    return [block(z_at)] + [z_swap(block(z_at ^ hop).astype(BF16), hop) for hop in (2, 3, 1)]


def gather_z(share):
    moved = {hop: z_swap(share, hop) for hop in (2, 3, 1)}
    return [share] + [moved[hop] for hop in (1, 2, 3)]


def join_z(slots, z_at):
    blocks = []
    for at in range(4):
        block = slots[at]
        for z in (1, 2, 3):
            block = jnp.where(z_at == z, slots[at ^ z], block)
        blocks.append(block)
    return jnp.concatenate(blocks, axis=1)


def on_device(tokens, gate_weight, up_weight, down_weight, grad_out):
    row = lax.axis_index("row")
    col = lax.axis_index("col")
    z_at, core = row // 2, row % 2
    at = jnp.stack([col // 8, col // 2 % 4, core])
    half = gate_weight.shape[1] // 2

    gate_t, up_t = gate_weight.T, up_weight.T
    joined = jnp.stack(
        [jnp.concatenate([gate_t[i * half : (i + 1) * half], up_t[i * half : (i + 1) * half]], axis=0) for i in range(2)]
    )
    in_mine = lax.dynamic_index_in_dim(joined, core, 0, keepdims=False)
    in_other = lax.dynamic_index_in_dim(joined, 1 - core, 0, keepdims=False)
    halves = down_weight.reshape(2, half, down_weight.shape[1])
    down_mine = lax.dynamic_index_in_dim(halves, core, 0, keepdims=False)
    down_other = lax.dynamic_index_in_dim(halves, 1 - core, 0, keepdims=False)

    def in_order(mine, other):
        return jnp.concatenate([jnp.where(core == 0, mine, other), jnp.where(core == 0, other, mine)], axis=0)

    def hi_cut(sums):
        middle = sums.shape[0] // 2
        return sums[:middle], sums[middle:].astype(BF16)

    tok_pair = jnp.concatenate([tokens, hi_swap(tokens)], axis=0)
    tok_line = jnp.stack(spread(tok_pair, 0))
    grad_out, tok_line = together(grad_out, tok_line)
    tok_lines, grad_hi = together(spread(tok_line, 1), hi_swap(grad_out))
    tok = join_xy(tok_lines, at)

    other = dot(in_other, tok, (1, 1))
    grad_pair, other = together(jnp.concatenate([grad_out, grad_hi], axis=0), other)
    grad_line, pre = together(spread(grad_pair, 0), dot(in_mine, tok, (1, 1)) + core_swap(other))
    grad_line, pre = together(jnp.stack(grad_line), pre)
    pre, grad_lines = scatter_z(pre, z_at), spread(grad_line, 1)
    grad = join_xy(grad_lines, at)
    other = dot(down_other, grad, (1, 1))
    pre, other = together(pre, other)
    pre = total(pre)
    gate_pre, up_pre = pre[:half], pre[half:]
    sigmoid_gate = jax.nn.sigmoid(gate_pre)
    hidden = (jax.nn.silu(gate_pre) * up_pre).astype(BF16)

    hidden_grad = dot(down_mine, grad, (1, 1)) + core_swap(other)
    hidden_grad, hid_mine = together(scatter_z(hidden_grad, z_at), gather_z(hidden))
    hidden_grad = total(hidden_grad)
    gate_delta = (hidden_grad * up_pre * sigmoid_gate * (1.0 + gate_pre * (1.0 - sigmoid_gate))).astype(BF16)
    up_delta = (hidden_grad * gate_pre * sigmoid_gate).astype(BF16)

    delta_mine = gather_z(jnp.concatenate([gate_delta, up_delta], axis=0))
    hid_mine = join_z(hid_mine, z_at)
    hid_other = core_swap(hid_mine)
    output = cut(dot(hid_mine, down_mine, (0, 0)) + dot(hid_other, down_other, (0, 0)), at)
    delta_mine, output = together(delta_mine, output)
    output = collect(output, 1)
    delta_mine = join_z(delta_mine, z_at)
    delta_other = core_swap(delta_mine)

    token_grad = cut(dot(delta_mine, in_mine, (0, 0)) + dot(delta_other, in_other, (0, 0)), at)
    token_grad, tok, grad = together(token_grad, tok, grad)
    token_grad = collect(token_grad, 1)
    output, token_grad[2] = together(output, token_grad[2])
    output = total(collect(cut_again(total(output), at), 0))

    down_grad = dot(in_order(hid_mine, hid_other), grad, (1, 0)).astype(BF16)
    gate_grad = dot(tok, in_order(delta_mine[:half], delta_other[:half]), (0, 1)).astype(BF16)
    up_grad = dot(tok, in_order(delta_mine[half:], delta_other[half:]), (0, 1)).astype(BF16)

    token_grad, down_grad, gate_grad, up_grad = together(token_grad, down_grad, gate_grad, up_grad)
    token_grad = total(collect(cut_again(total(token_grad), at), 0))
    own, other = zip(hi_cut(output), hi_cut(token_grad))
    other = hi_swap(jnp.stack(other)).astype(F32)
    output, token_grad = (own[0] + other[0]).astype(BF16), (own[1] + other[1]).astype(BF16)
    return output, token_grad, gate_grad, up_grad, down_grad


def solution(mesh):
    by_token, by_hidden = P("col", "row"), P("row", "col")
    return jax.shard_map(
        on_device,
        mesh=mesh,
        in_specs=(by_token, by_hidden, by_hidden, by_token, by_token),
        out_specs=(by_token, by_token, by_hidden, by_hidden, by_token),
        check_vma=False,
    )
```

```python
import jax
import jax.numpy as jnp
from jax import lax
from jax.experimental import pallas as pl
from jax.experimental.pallas import tpu as pltpu
from jax.sharding import PartitionSpec as P

F32 = jnp.float32
BF16 = jnp.bfloat16

HI_SWAP = [(i, i ^ 1) for i in range(32)]
CORE_SWAP = [(i, i ^ 1) for i in range(8)]


def dot(left, right, dims):
    return lax.dot_general(left, right, ((dims[:1], dims[1:]), ((), ())), preferred_element_type=F32)


def together(*values):
    return lax.optimization_barrier(values)


def core_swap(value):
    return lax.ppermute(value, "row", CORE_SWAP)


def hi_swap(value):
    return lax.ppermute(value, "col", HI_SWAP)


def z_swap(value, hop):
    return lax.ppermute(value, "row", [(i, i ^ (2 * hop)) for i in range(8)])


def xy_move(value, hop, core_on_x):
    pairs = []
    for row in range(8):
        for x in range(4):
            for y in range(4):
                to_x, to_y = ((x + hop) % 4, y) if row % 2 == core_on_x else (x, (y + hop) % 4)
                for hi in range(2):
                    pairs.append((row * 32 + (x * 4 + y) * 2 + hi, row * 32 + (to_x * 4 + to_y) * 2 + hi))
    return lax.ppermute(value, ("row", "col"), pairs)


def spread(value, core_on_x):
    moved = {hop: xy_move(value, hop, core_on_x) for hop in (2, 1, 3)}
    return [value] + [moved[hop] for hop in (1, 2, 3)]


def place_kernel(at, *refs):
    *lines, out = refs
    x, y, core = at[0], at[1], at[2]
    for e in range(4):
        for d in range(4):
            from_x = lax.rem(x + 4 - jnp.where(core == 1, e, d), 4)
            from_y = lax.rem(y + 4 - jnp.where(core == 1, d, e), 4)
            out[from_x * 4 + from_y] = lines[e][d]


def join_xy(lines, at):
    _, t, d = lines[0].shape
    out = pl.pallas_call(
        place_kernel,
        out_shape=jax.ShapeDtypeStruct((16, t, d), lines[0].dtype),
        in_specs=[pl.BlockSpec(memory_space=pltpu.SMEM)] + [pl.BlockSpec(memory_space=pltpu.VMEM)] * 4,
        out_specs=pl.BlockSpec(memory_space=pltpu.VMEM),
        compiler_params=pltpu.CompilerParams(vmem_limit_bytes=16 * 1024 * 1024),
        cost_estimate=pl.CostEstimate(flops=0, bytes_accessed=64 * t * d, transcendentals=0),
    )(at, *lines)
    return out.reshape(16 * t, d)


def cut(partial, at):
    blocks = partial.reshape(4, 4, -1, partial.shape[1])

    def piece(hop):
        along_x = lax.dynamic_index_in_dim(blocks, (at[0] + 4 - hop) % 4, 0, keepdims=False)
        along_y = lax.dynamic_index_in_dim(blocks, (at[1] + 4 - hop) % 4, 1, keepdims=False)
        return jnp.where(at[2] == 1, along_x, along_y)

    return [piece(0)] + [piece(hop).astype(BF16) for hop in (1, 2, 3)]


def cut_again(sums, at):
    place = jnp.where(at[2] == 1, at[1], at[0])
    pieces = [lax.dynamic_index_in_dim(sums, (place + 4 - hop) % 4, 1, keepdims=False) for hop in range(4)]
    return [pieces[0]] + [piece.astype(BF16) for piece in pieces[1:]]


def collect(pieces, core_on_x):
    moved = {hop: xy_move(pieces[hop].astype(BF16), -hop, core_on_x) for hop in (2, 1, 3)}
    return [pieces[0]] + [moved[hop] for hop in (1, 2, 3)]


def total(parts):
    return parts[0] + parts[1].astype(F32) + parts[2].astype(F32) + parts[3].astype(F32)


def z_blocks(both, z_at):
    width = both.shape[1] // 4

    def block(at):
        return lax.dynamic_slice_in_dim(both, at * width, width, axis=1)

    return [block(z_at)] + [block(z_at ^ hop).astype(BF16) for hop in (1, 2, 3)]


def scatter_z(blocks):
    moved = {hop: z_swap(blocks[hop], hop) for hop in (2, 3, 1)}
    return [blocks[0]] + [moved[hop] for hop in (1, 2, 3)]


def gather_z(share):
    moved = {hop: z_swap(share, hop) for hop in (2, 3, 1)}
    return [share] + [moved[hop] for hop in (1, 2, 3)]


def join_kernel(at, *refs):
    *slots, out = refs
    width = slots[0].shape[1]
    for hop in range(4):
        place = jnp.bitwise_xor(at[3], hop)
        out[:, pl.ds(pl.multiple_of(place * width, width), width)] = slots[hop][...]


def join_z(slots, at):
    r, width = slots[0].shape
    return pl.pallas_call(
        join_kernel,
        out_shape=jax.ShapeDtypeStruct((r, 4 * width), slots[0].dtype),
        in_specs=[pl.BlockSpec(memory_space=pltpu.SMEM)] + [pl.BlockSpec(memory_space=pltpu.VMEM)] * 4,
        out_specs=pl.BlockSpec(memory_space=pltpu.VMEM),
        compiler_params=pltpu.CompilerParams(vmem_limit_bytes=16 * 1024 * 1024),
        cost_estimate=pl.CostEstimate(flops=0, bytes_accessed=16 * r * width, transcendentals=0),
    )(at, *slots)


def on_device(tokens, gate_weight, up_weight, down_weight, grad_out):
    row = lax.axis_index("row")
    col = lax.axis_index("col")
    z_at, core = row // 2, row % 2
    at = jnp.stack([col // 8, col // 2 % 4, core, z_at])
    half = gate_weight.shape[1] // 2

    gate_t, up_t = gate_weight.T, up_weight.T
    joined = jnp.stack(
        [jnp.concatenate([gate_t[i * half : (i + 1) * half], up_t[i * half : (i + 1) * half]], axis=0) for i in range(2)]
    )
    in_mine = lax.dynamic_index_in_dim(joined, core, 0, keepdims=False)
    in_other = lax.dynamic_index_in_dim(joined, 1 - core, 0, keepdims=False)
    halves = down_weight.reshape(2, half, down_weight.shape[1])
    down_mine = lax.dynamic_index_in_dim(halves, core, 0, keepdims=False)
    down_other = lax.dynamic_index_in_dim(halves, 1 - core, 0, keepdims=False)

    def in_order(mine, other):
        return jnp.concatenate([jnp.where(core == 0, mine, other), jnp.where(core == 0, other, mine)], axis=0)

    tok_pair = jnp.concatenate([tokens, hi_swap(tokens)], axis=0)
    tok_line = jnp.stack(spread(tok_pair, 0))
    grad_out, tok_line = together(grad_out, tok_line)
    tok_lines, grad_hi = together(spread(tok_line, 1), hi_swap(grad_out))
    tok = join_xy(tok_lines, at)

    other = dot(in_other, tok, (1, 1))
    grad_pair, other = together(jnp.concatenate([grad_out, grad_hi], axis=0), other)
    grad_line, pre = together(spread(grad_pair, 0), dot(in_mine, tok, (1, 1)) + core_swap(other))
    grad_line, pre = together(jnp.stack(grad_line), pre)
    pre, grad_lines = scatter_z(z_blocks(pre, z_at)), spread(grad_line, 1)
    grad = join_xy(grad_lines, at)
    other = dot(down_other, grad, (1, 1))
    pre, other = together(pre, other)
    pre = total(pre)
    gate_pre, up_pre = pre[:half], pre[half:]
    sigmoid_gate = jax.nn.sigmoid(gate_pre)
    hidden = (jax.nn.silu(gate_pre) * up_pre).astype(BF16)

    hidden_grad = dot(down_mine, grad, (1, 1)) + core_swap(other)
    hidden_grad, hid_mine = together(scatter_z(z_blocks(hidden_grad, z_at)), gather_z(hidden))
    hidden_grad = total(hidden_grad)
    gate_delta = (hidden_grad * up_pre * sigmoid_gate * (1.0 + gate_pre * (1.0 - sigmoid_gate))).astype(BF16)
    up_delta = (hidden_grad * gate_pre * sigmoid_gate).astype(BF16)

    delta_mine = gather_z(jnp.concatenate([gate_delta, up_delta], axis=0))
    hid_mine = join_z(hid_mine, at)
    hid_other = core_swap(hid_mine)
    output = cut(dot(hid_mine, down_mine, (0, 0)) + dot(hid_other, down_other, (0, 0)), at)
    delta_mine, output = together(delta_mine, output)
    output = collect(output, 1)
    delta_mine = join_z(delta_mine, at)
    delta_other = core_swap(delta_mine)

    token_grad = cut(dot(delta_mine, in_mine, (0, 0)) + dot(delta_other, in_other, (0, 0)), at)
    token_grad, tok, grad = together(token_grad, tok, grad)
    token_grad = collect(token_grad, 1)
    output, token_grad[2] = together(output, token_grad[2])

    down_grad = dot(in_order(hid_mine, hid_other), grad, (1, 0)).astype(BF16)
    gate_grad = dot(tok, in_order(delta_mine[:half], delta_other[:half]), (0, 1)).astype(BF16)
    up_grad = dot(tok, in_order(delta_mine[half:], delta_other[half:]), (0, 1)).astype(BF16)

    token_grad, output, down_grad, gate_grad, up_grad = together(token_grad, total(output), down_grad, gate_grad, up_grad)
    sums = total(collect(cut_again(jnp.stack([output, total(token_grad)]), at), 0))
    middle = sums.shape[1] // 2
    other = hi_swap(sums[:, middle:].astype(BF16))
    output, token_grad = (sums[:, :middle] + other.astype(F32)).astype(BF16)
    return output, token_grad, gate_grad, up_grad, down_grad


def solution(mesh):
    by_token, by_hidden = P("col", "row"), P("row", "col")
    return jax.shard_map(
        on_device,
        mesh=mesh,
        in_specs=(by_token, by_hidden, by_hidden, by_token, by_token),
        out_specs=(by_token, by_token, by_hidden, by_hidden, by_token),
        check_vma=False,
    )
```

```python
import jax
import jax.numpy as jnp
from jax import lax
from jax.experimental import pallas as pl
from jax.experimental.pallas import tpu as pltpu
from jax.sharding import PartitionSpec as P

F32 = jnp.float32
BF16 = jnp.bfloat16

HI_SWAP = [(i, i ^ 1) for i in range(32)]
CORE_SWAP = [(i, i ^ 1) for i in range(8)]


def dot(left, right, dims):
    return lax.dot_general(left, right, ((dims[:1], dims[1:]), ((), ())), preferred_element_type=F32)


def together(*values):
    return lax.optimization_barrier(values)


def core_swap(value):
    return lax.ppermute(value, "row", CORE_SWAP)


def hi_swap(value):
    return lax.ppermute(value, "col", HI_SWAP)


def z_swap(value, hop):
    return lax.ppermute(value, "row", [(i, i ^ (2 * hop)) for i in range(8)])


def xy_move(value, hop, core_on_x):
    pairs = []
    for row in range(8):
        for x in range(4):
            for y in range(4):
                to_x, to_y = ((x + hop) % 4, y) if row % 2 == core_on_x else (x, (y + hop) % 4)
                for hi in range(2):
                    pairs.append((row * 32 + (x * 4 + y) * 2 + hi, row * 32 + (to_x * 4 + to_y) * 2 + hi))
    return lax.ppermute(value, ("row", "col"), pairs)


def spread(value, core_on_x):
    moved = {hop: xy_move(value, hop, core_on_x) for hop in (1, 3, 2)}
    return [value] + [moved[hop] for hop in (1, 2, 3)]


def place_kernel(at, *refs):
    *lines, out = refs
    x, y, core = at[0], at[1], at[2]
    for e in range(4):
        for d in range(4):
            from_x = lax.rem(x + 4 - jnp.where(core == 1, e, d), 4)
            from_y = lax.rem(y + 4 - jnp.where(core == 1, d, e), 4)
            out[from_x * 4 + from_y] = lines[e][d]


def join_xy(lines, at):
    _, t, d = lines[0].shape
    out = pl.pallas_call(
        place_kernel,
        out_shape=jax.ShapeDtypeStruct((16, t, d), lines[0].dtype),
        in_specs=[pl.BlockSpec(memory_space=pltpu.SMEM)] + [pl.BlockSpec(memory_space=pltpu.VMEM)] * 4,
        out_specs=pl.BlockSpec(memory_space=pltpu.VMEM),
        compiler_params=pltpu.CompilerParams(vmem_limit_bytes=16 * 1024 * 1024),
        cost_estimate=pl.CostEstimate(flops=0, bytes_accessed=64 * t * d, transcendentals=0),
    )(at, *lines)
    return out.reshape(16 * t, d)


def cut(partial, at):
    blocks = partial.reshape(4, 4, -1, partial.shape[1])

    def piece(hop):
        along_x = lax.dynamic_index_in_dim(blocks, (at[0] + 4 - hop) % 4, 0, keepdims=False)
        along_y = lax.dynamic_index_in_dim(blocks, (at[1] + 4 - hop) % 4, 1, keepdims=False)
        return jnp.where(at[2] == 1, along_x, along_y)

    return [piece(0)] + [piece(hop).astype(BF16) for hop in (1, 2, 3)]


def cut_again(sums, at):
    place = jnp.where(at[2] == 1, at[1], at[0])
    pieces = [lax.dynamic_index_in_dim(sums, (place + 4 - hop) % 4, 1, keepdims=False) for hop in range(4)]
    return [pieces[0]] + [piece.astype(BF16) for piece in pieces[1:]]


def collect(pieces, core_on_x):
    moved = {hop: xy_move(pieces[hop].astype(BF16), -hop, core_on_x) for hop in (1, 3, 2)}
    return [pieces[0]] + [moved[hop] for hop in (1, 2, 3)]


def total(parts):
    return parts[0] + parts[1].astype(F32) + parts[2].astype(F32) + parts[3].astype(F32)


def z_blocks(both, z_at):
    width = both.shape[1] // 4

    def block(at):
        return lax.dynamic_slice_in_dim(both, at * width, width, axis=1)

    return [block(z_at)] + [block(z_at ^ hop).astype(BF16) for hop in (1, 2, 3)]


def scatter_z(blocks):
    moved = {hop: z_swap(blocks[hop], hop) for hop in (2, 3, 1)}
    return [blocks[0]] + [moved[hop] for hop in (1, 2, 3)]


def gather_z(share):
    moved = {hop: z_swap(share, hop) for hop in (2, 3, 1)}
    return [share] + [moved[hop] for hop in (1, 2, 3)]


def join_kernel(at, *refs):
    *slots, out = refs
    width = slots[0].shape[1]
    for hop in range(4):
        place = jnp.bitwise_xor(at[3], hop)
        out[:, pl.ds(pl.multiple_of(place * width, width), width)] = slots[hop][...]


def join_z(slots, at):
    r, width = slots[0].shape
    return pl.pallas_call(
        join_kernel,
        out_shape=jax.ShapeDtypeStruct((r, 4 * width), slots[0].dtype),
        in_specs=[pl.BlockSpec(memory_space=pltpu.SMEM)] + [pl.BlockSpec(memory_space=pltpu.VMEM)] * 4,
        out_specs=pl.BlockSpec(memory_space=pltpu.VMEM),
        compiler_params=pltpu.CompilerParams(vmem_limit_bytes=16 * 1024 * 1024),
        cost_estimate=pl.CostEstimate(flops=0, bytes_accessed=16 * r * width, transcendentals=0),
    )(at, *slots)


def on_device(tokens, gate_weight, up_weight, down_weight, grad_out):
    row = lax.axis_index("row")
    col = lax.axis_index("col")
    z_at, core = row // 2, row % 2
    at = jnp.stack([col // 8, col // 2 % 4, core, z_at])
    half = gate_weight.shape[1] // 2

    gate_t, up_t = gate_weight.T, up_weight.T
    joined = jnp.stack(
        [jnp.concatenate([gate_t[i * half : (i + 1) * half], up_t[i * half : (i + 1) * half]], axis=0) for i in range(2)]
    )
    in_mine = lax.dynamic_index_in_dim(joined, core, 0, keepdims=False)
    in_other = lax.dynamic_index_in_dim(joined, 1 - core, 0, keepdims=False)
    halves = down_weight.reshape(2, half, down_weight.shape[1])
    down_mine = lax.dynamic_index_in_dim(halves, core, 0, keepdims=False)
    down_other = lax.dynamic_index_in_dim(halves, 1 - core, 0, keepdims=False)

    def in_order(mine, other):
        return jnp.concatenate([jnp.where(core == 0, mine, other), jnp.where(core == 0, other, mine)], axis=0)

    tok_pair = jnp.concatenate([tokens, hi_swap(tokens)], axis=0)
    tok_line = jnp.stack(spread(tok_pair, 0))
    grad_out, tok_line = together(grad_out, tok_line)
    tok_lines, grad_hi = together(spread(tok_line, 1), hi_swap(grad_out))
    tok = join_xy(tok_lines, at)

    other = dot(in_other, tok, (1, 1))
    grad_pair, other = together(jnp.concatenate([grad_out, grad_hi], axis=0), other)
    grad_line, pre = together(spread(grad_pair, 0), dot(in_mine, tok, (1, 1)) + core_swap(other))
    pre = z_blocks(pre, z_at)
    grad_line, pre = together(grad_line, pre)
    pre, grad_lines = scatter_z(pre), spread(jnp.stack(grad_line), 1)
    grad = join_xy(grad_lines, at)
    other = dot(down_other, grad, (1, 1))
    pre, other = together(pre, other)
    pre = total(pre)
    gate_pre, up_pre = pre[:half], pre[half:]
    sigmoid_gate = jax.nn.sigmoid(gate_pre)
    hidden = (jax.nn.silu(gate_pre) * up_pre).astype(BF16)

    hidden_grad = dot(down_mine, grad, (1, 1)) + core_swap(other)
    hidden_grad, hid_mine = together(scatter_z(z_blocks(hidden_grad, z_at)), gather_z(hidden))
    hidden_grad = total(hidden_grad)
    gate_delta = (hidden_grad * up_pre * sigmoid_gate * (1.0 + gate_pre * (1.0 - sigmoid_gate))).astype(BF16)
    up_delta = (hidden_grad * gate_pre * sigmoid_gate).astype(BF16)

    delta_mine = gather_z(jnp.concatenate([gate_delta, up_delta], axis=0))
    hid_mine = join_z(hid_mine, at)
    hid_other = core_swap(hid_mine)
    output = cut(dot(hid_mine, down_mine, (0, 0)) + dot(hid_other, down_other, (0, 0)), at)
    delta_mine, output = together(delta_mine, output)
    output = collect(output, 1)
    delta_mine = join_z(delta_mine, at)
    delta_other = core_swap(delta_mine)

    token_grad = cut(dot(delta_mine, in_mine, (0, 0)) + dot(delta_other, in_other, (0, 0)), at)
    token_grad, tok, grad = together(token_grad, tok, grad)
    token_grad = collect(token_grad, 1)
    output, token_grad[2] = together(output, token_grad[2])

    down_grad = dot(in_order(hid_mine, hid_other), grad, (1, 0)).astype(BF16)
    gate_grad = dot(tok, in_order(delta_mine[:half], delta_other[:half]), (0, 1)).astype(BF16)
    up_grad = dot(tok, in_order(delta_mine[half:], delta_other[half:]), (0, 1)).astype(BF16)

    token_grad, output, down_grad, gate_grad, up_grad = together(token_grad, total(output), down_grad, gate_grad, up_grad)
    sums = total(collect(cut_again(jnp.stack([output, total(token_grad)]), at), 0))
    middle = sums.shape[1] // 2
    other = hi_swap(sums[:, middle:].astype(BF16))
    output, token_grad = (sums[:, :middle] + other.astype(F32)).astype(BF16)
    return output, token_grad, gate_grad, up_grad, down_grad


def solution(mesh):
    by_token, by_hidden = P("col", "row"), P("row", "col")
    return jax.shard_map(
        on_device,
        mesh=mesh,
        in_specs=(by_token, by_hidden, by_hidden, by_token, by_token),
        out_specs=(by_token, by_token, by_hidden, by_hidden, by_token),
        check_vma=False,
    )
```

```python
import jax
import jax.numpy as jnp
from jax import lax
from jax.experimental import pallas as pl
from jax.experimental.pallas import tpu as pltpu
from jax.sharding import PartitionSpec as P

F32 = jnp.float32
BF16 = jnp.bfloat16

HI_SWAP = [(i, i ^ 1) for i in range(32)]
CORE_SWAP = [(i, i ^ 1) for i in range(8)]


def dot(left, right, dims):
    return lax.dot_general(left, right, ((dims[:1], dims[1:]), ((), ())), preferred_element_type=F32)


def together(*values):
    return lax.optimization_barrier(values)


def core_swap(value):
    return lax.ppermute(value, "row", CORE_SWAP)


def hi_swap(value):
    return lax.ppermute(value, "col", HI_SWAP)


def z_swap(value, hop):
    return lax.ppermute(value, "row", [(i, i ^ (2 * hop)) for i in range(8)])


def xy_move(value, hop, core_on_x):
    pairs = []
    for row in range(8):
        for x in range(4):
            for y in range(4):
                to_x, to_y = ((x + hop) % 4, y) if row % 2 == core_on_x else (x, (y + hop) % 4)
                for hi in range(2):
                    pairs.append((row * 32 + (x * 4 + y) * 2 + hi, row * 32 + (to_x * 4 + to_y) * 2 + hi))
    return lax.ppermute(value, ("row", "col"), pairs)


def spread(value, core_on_x):
    moved = {hop: xy_move(value, hop, core_on_x) for hop in (1, 3, 2)}
    return [value] + [moved[hop] for hop in (1, 2, 3)]


def place_kernel(at, *refs):
    *lines, out = refs
    x, y, core = at[0], at[1], at[2]
    for e in range(4):
        for d in range(4):
            from_x = lax.rem(x + 4 - jnp.where(core == 1, e, d), 4)
            from_y = lax.rem(y + 4 - jnp.where(core == 1, d, e), 4)
            out[from_x * 4 + from_y] = lines[e][d]


def join_xy(lines, at):
    _, t, d = lines[0].shape
    out = pl.pallas_call(
        place_kernel,
        out_shape=jax.ShapeDtypeStruct((16, t, d), lines[0].dtype),
        in_specs=[pl.BlockSpec(memory_space=pltpu.SMEM)] + [pl.BlockSpec(memory_space=pltpu.VMEM)] * 4,
        out_specs=pl.BlockSpec(memory_space=pltpu.VMEM),
        compiler_params=pltpu.CompilerParams(vmem_limit_bytes=16 * 1024 * 1024),
        cost_estimate=pl.CostEstimate(flops=0, bytes_accessed=64 * t * d, transcendentals=0),
    )(at, *lines)
    return out.reshape(16 * t, d)


def cut(partial, at):
    blocks = partial.reshape(4, 4, -1, partial.shape[1])

    def piece(hop):
        along_x = lax.dynamic_index_in_dim(blocks, (at[0] + 4 - hop) % 4, 0, keepdims=False)
        along_y = lax.dynamic_index_in_dim(blocks, (at[1] + 4 - hop) % 4, 1, keepdims=False)
        return jnp.where(at[2] == 1, along_x, along_y)

    return [piece(0)] + [piece(hop).astype(BF16) for hop in (1, 2, 3)]


def cut_again(sums, at):
    place = jnp.where(at[2] == 1, at[1], at[0])
    pieces = [lax.dynamic_index_in_dim(sums, (place + 4 - hop) % 4, 1, keepdims=False) for hop in range(4)]
    return [pieces[0]] + [piece.astype(BF16) for piece in pieces[1:]]


def collect(pieces, core_on_x):
    moved = {hop: xy_move(pieces[hop].astype(BF16), -hop, core_on_x) for hop in (1, 3, 2)}
    return [pieces[0]] + [moved[hop] for hop in (1, 2, 3)]


def total(parts):
    return parts[0] + parts[1].astype(F32) + parts[2].astype(F32) + parts[3].astype(F32)


def z_blocks(both, z_at):
    width = both.shape[1] // 4

    def block(at):
        return lax.dynamic_slice_in_dim(both, at * width, width, axis=1)

    return [block(z_at)] + [block(z_at ^ hop).astype(BF16) for hop in (1, 2, 3)]


def scatter_z(blocks):
    moved = {hop: z_swap(blocks[hop], hop) for hop in (2, 3, 1)}
    return [blocks[0]] + [moved[hop] for hop in (1, 2, 3)]


def gather_z(share):
    moved = {hop: z_swap(share, hop) for hop in (2, 3, 1)}
    return [share] + [moved[hop] for hop in (1, 2, 3)]


def join_kernel(at, *refs):
    *slots, out = refs
    width = slots[0].shape[1]
    for hop in range(4):
        place = jnp.bitwise_xor(at[3], hop)
        out[:, pl.ds(pl.multiple_of(place * width, width), width)] = slots[hop][...]


def join_z(slots, at):
    r, width = slots[0].shape
    return pl.pallas_call(
        join_kernel,
        out_shape=jax.ShapeDtypeStruct((r, 4 * width), slots[0].dtype),
        in_specs=[pl.BlockSpec(memory_space=pltpu.SMEM)] + [pl.BlockSpec(memory_space=pltpu.VMEM)] * 4,
        out_specs=pl.BlockSpec(memory_space=pltpu.VMEM),
        compiler_params=pltpu.CompilerParams(vmem_limit_bytes=16 * 1024 * 1024),
        cost_estimate=pl.CostEstimate(flops=0, bytes_accessed=16 * r * width, transcendentals=0),
    )(at, *slots)


def on_device(tokens, gate_weight, up_weight, down_weight, grad_out):
    row = lax.axis_index("row")
    col = lax.axis_index("col")
    z_at, core = row // 2, row % 2
    at = jnp.stack([col // 8, col // 2 % 4, core, z_at])
    half = gate_weight.shape[1] // 2

    gate_t, up_t = gate_weight.T, up_weight.T
    joined = jnp.stack(
        [jnp.concatenate([gate_t[i * half : (i + 1) * half], up_t[i * half : (i + 1) * half]], axis=0) for i in range(2)]
    )
    in_mine = lax.dynamic_index_in_dim(joined, core, 0, keepdims=False)
    in_other = lax.dynamic_index_in_dim(joined, 1 - core, 0, keepdims=False)
    halves = down_weight.reshape(2, half, down_weight.shape[1])
    down_mine = lax.dynamic_index_in_dim(halves, core, 0, keepdims=False)
    down_other = lax.dynamic_index_in_dim(halves, 1 - core, 0, keepdims=False)
    down_all = jnp.concatenate([down_mine, down_other], axis=0)

    def in_order(mine, other):
        return jnp.concatenate([jnp.where(core == 0, mine, other), jnp.where(core == 0, other, mine)], axis=0)

    tok_pair = jnp.concatenate([tokens, hi_swap(tokens)], axis=0)
    tok_line = jnp.stack(spread(tok_pair, 0))
    grad_out, tok_line = together(grad_out, tok_line)
    tok_lines, grad_hi = together(spread(tok_line, 1), hi_swap(grad_out))
    tok = join_xy(tok_lines, at)

    other = dot(in_other, tok, (1, 1))
    grad_pair, other = together(jnp.concatenate([grad_out, grad_hi], axis=0), other)
    grad_line, pre = together(spread(grad_pair, 0), dot(in_mine, tok, (1, 1)) + core_swap(other))
    pre = z_blocks(pre, z_at)
    grad_line, pre = together(grad_line, pre)
    pre, grad_lines = scatter_z(pre), spread(jnp.stack(grad_line), 1)
    grad = join_xy(grad_lines, at)
    other = dot(down_other, grad, (1, 1))
    pre, other = together(pre, other)
    pre = total(pre)
    gate_pre, up_pre = pre[:half], pre[half:]
    sigmoid_gate = jax.nn.sigmoid(gate_pre)
    hidden = (jax.nn.silu(gate_pre) * up_pre).astype(BF16)

    hidden_grad = dot(down_mine, grad, (1, 1)) + core_swap(other)
    hidden_grad, hid_mine = together(scatter_z(z_blocks(hidden_grad, z_at)), gather_z(hidden))
    hidden_grad = total(hidden_grad)
    gate_delta = (hidden_grad * up_pre * sigmoid_gate * (1.0 + gate_pre * (1.0 - sigmoid_gate))).astype(BF16)
    up_delta = (hidden_grad * gate_pre * sigmoid_gate).astype(BF16)

    delta_mine = gather_z(jnp.concatenate([gate_delta, up_delta], axis=0))
    hid_mine = join_z(hid_mine, at)
    hid_other = core_swap(hid_mine)
    output = cut(dot(jnp.concatenate([hid_mine, hid_other], axis=0), down_all, (0, 0)), at)
    delta_mine, output[1], output[3] = together(delta_mine, output[1], output[3])
    output = collect(output, 1)
    delta_mine = join_z(delta_mine, at)
    delta_other = core_swap(delta_mine)

    token_grad = cut(dot(delta_mine, in_mine, (0, 0)) + dot(delta_other, in_other, (0, 0)), at)
    token_grad, tok, grad = together(token_grad, tok, grad)
    token_grad = collect(token_grad, 1)
    output, token_grad[2] = together(output, token_grad[2])

    down_grad = dot(in_order(hid_mine, hid_other), grad, (1, 0)).astype(BF16)
    gate_grad = dot(tok, in_order(delta_mine[:half], delta_other[:half]), (0, 1)).astype(BF16)
    up_grad = dot(tok, in_order(delta_mine[half:], delta_other[half:]), (0, 1)).astype(BF16)

    token_grad, output, down_grad, gate_grad, up_grad = together(token_grad, total(output), down_grad, gate_grad, up_grad)
    sums = total(collect(cut_again(jnp.stack([output, total(token_grad)]), at), 0))
    middle = sums.shape[1] // 2
    other = hi_swap(sums[:, middle:].astype(BF16))
    output, token_grad = (sums[:, :middle] + other.astype(F32)).astype(BF16)
    return output, token_grad, gate_grad, up_grad, down_grad


def solution(mesh):
    by_token, by_hidden = P("col", "row"), P("row", "col")
    return jax.shard_map(
        on_device,
        mesh=mesh,
        in_specs=(by_token, by_hidden, by_hidden, by_token, by_token),
        out_specs=(by_token, by_token, by_hidden, by_hidden, by_token),
        check_vma=False,
    )
```
